256 devices in a mesh: blk: 32 (over x_lo, z, core), depth: 8 (over y, x_hi).
Axes of the slice: x: 4 (x_hi: 2, x_lo: 2; x = x_hi * 2 + x_lo), y: 4, z: 8, core: 2. Of those that a mesh axis runs over, the one named last changes fastest.
Arguments:
- picture_features: float32 [16384, 1152], P(('blk', 'depth')), may hold values from -2 to 2
- caption_features: float32 [16384, 1152], P(('blk', 'depth')), may hold values from -2 to 2
- scale_exponent: float32 [1], replicated, may hold values from 2 to 2.6
- similarity_intercept: float32 [1], replicated, may hold values from -7 to -5
Outputs:
- image_gradient: float32 [16384, 1152], P(('blk', 'depth'))
- wording_loss_derivative: float32 [16384, 1152], P(('blk', 'depth'))
The draws below stay inside these ranges and needn't reach their ends.
All inputs are finite; a program needn't handle non-finite values.
Results may differ from the reference program's by a relative error of at most 0.0003.
Values sent between devices are 32-bit elements; how exact they have to be, the bound alone decides.
No kernel may reach another device: no remote copies, remote signals or barrier semaphores. Data moves between devices by JAX's collectives and lax.ppermute only.
A program may use at most 64 MiB of HBM per device.

```python
import jax
import jax.numpy as jnp
from jax import lax

D = 1152
PAIR_DEV = 64
BATCH = 16384
N_DEPTH = 8


def paired_part(key):
    return jax.random.truncated_normal(jax.random.fold_in(key, 5), -4.0, 4.0, (BATCH, D), jnp.float32)


def scaled_rows(subkeys, shared, private):
    row_scale = jnp.exp(jax.random.uniform(subkeys[1], (BATCH, 1), jnp.float32, -1.15, 1.15))
    column_scale = jnp.exp(jax.random.uniform(subkeys[2], (1, D), jnp.float32, -1.15, 1.15))
    mixture = 0.7 * shared + private
    return jnp.clip(mixture * column_scale * row_scale / jnp.sqrt(3.2 * D), -2.0, 2.0)


def draw_picture_features(key, part):
    shared = paired_part(key)
    key = jax.random.fold_in(key, 11)
    subkeys = jax.random.split(key, 4)
    private = jax.random.truncated_normal(subkeys[0], -4.0, 4.0, (BATCH, D), jnp.float32)
    return scaled_rows(subkeys, shared, private)


def draw_caption_features(key, part):
    shared = paired_part(key)
    key = jax.random.fold_in(key, 12)
    subkeys = jax.random.split(key, 4)
    private = jax.random.truncated_normal(subkeys[0], -4.0, 4.0, (BATCH, D), jnp.float32)
    return scaled_rows(subkeys, shared, private)


def setup_inputs(seed: int = 0) -> dict:
    arg_keys = jax.random.split(jax.random.key(seed), 5)
    picture_features = draw_picture_features(jax.random.fold_in(arg_keys[4], 71), 0)
    caption_features = draw_caption_features(jax.random.fold_in(arg_keys[4], 71), 0)
    scale_exponent = jnp.clip(jax.random.uniform(arg_keys[2], (1,), jnp.float32, 2.0, 2.6), 2.0, 2.6)
    similarity_intercept = jnp.clip(jax.random.uniform(arg_keys[3], (1,), jnp.float32, -7.0, -5.0), -7.0, -5.0)
    return {"picture_features": picture_features, "caption_features": caption_features, "scale_exponent": scale_exponent, "similarity_intercept": similarity_intercept}


EPSILON = 1e-06

def normalize(embed):
    inverse = lax.rsqrt(lax.optimization_barrier(jnp.sum(embed * embed, axis=1, keepdims=True)) + EPSILON)
    return (embed * inverse, inverse)

def back_through(unit_rows, inverse, direction):
    along = lax.optimization_barrier(jnp.sum(unit_rows * direction, axis=1, keepdims=True))
    return inverse * (direction - unit_rows * along)

def reference(picture_features, caption_features, scale_exponent, similarity_intercept):
    similarity_multiplier = jnp.exp(scale_exponent[0])
    image_unit, image_inverse = normalize(picture_features)
    caption_unitlength, text_inverse = normalize(caption_features)
    block_size = PAIR_DEV * N_DEPTH
    count_blocks = BATCH // block_size
    text_index = jnp.arange(BATCH, dtype=jnp.int32)
    finest_accuracy = lax.Precision.HIGHEST

    def visit(carried, block_index):
        first_row = block_index * block_size
        picture_entry_group = lax.dynamic_slice_in_dim(image_unit, first_row, block_size, 0)
        score_table = similarity_multiplier * lax.dot_general(picture_entry_group, caption_unitlength, (((1,), (1,)), ((), ())), precision=finest_accuracy, preferred_element_type=jnp.float32) + similarity_intercept[0]
        row_index = first_row + jnp.arange(block_size, dtype=jnp.int32)
        label_sign = jnp.where(row_index[:, None] == text_index[None, :], 1.0, -1.0).astype(jnp.float32)
        logistic_derivs = -label_sign * jax.nn.sigmoid(-label_sign * score_table)
        picture_share = similarity_multiplier * jnp.dot(logistic_derivs, caption_unitlength, precision=finest_accuracy, preferred_element_type=jnp.float32)
        caption_share = similarity_multiplier * lax.dot_general(logistic_derivs, picture_entry_group, (((0,), (0,)), ((), ())), precision=finest_accuracy, preferred_element_type=jnp.float32)
        return (carried + caption_share, picture_share)
    text_dir, image_blocks = lax.scan(visit, jnp.zeros((BATCH, D), jnp.float32), jnp.arange(count_blocks, dtype=jnp.int32))
    image_dir = image_blocks.reshape(BATCH, D)
    return (back_through(image_unit, image_inverse, image_dir), back_through(caption_unitlength, text_inverse, text_dir))
```

```python
import functools

import jax
import jax.numpy as jnp
from jax import lax
from jax.experimental import pallas as pl
from jax.experimental.pallas import tpu as pltpu
from jax.sharding import Mesh, PartitionSpec as P

EPSILON = 1e-06
D = 1152
ROWS = 64
HALF = 32
BUNDLE = 128
SIDE = 1024
NEAR = 512
PAIR = 256
VMEM_LIMIT = 56 * 1024 * 1024
F32 = jnp.float32
BF16 = jnp.bfloat16
ROWS_ROWS = (((0,), (0,)), ((), ()))
FEATURES = (((1,), (1,)), ((), ()))
PLAIN = (((1,), (0,)), ((), ()))
RING_X = ("xl", "xh")


def x_index(place):
    return (place % 2) * 2 + place // 2


def shift_x(value, by):
    return lax.ppermute(value, RING_X, [(x_index(i), x_index((i + by) % 4)) for i in range(4)])


def shift_y(value, by):
    return lax.ppermute(value, "y", [(i, (i + by) % 4) for i in range(4)])


def swap_core(value):
    return lax.ppermute(value, "core", [(0, 1), (1, 0)])


def split(value):
    high = value.astype(BF16)
    low = (value - high.astype(F32)).astype(BF16)
    return high, low


def dot3(left, right, dims):
    dot = functools.partial(lax.dot_general, dimension_numbers=dims, preferred_element_type=F32)
    return dot(left[0], right[0]) + (dot(left[0], right[1]) + dot(left[1], right[0]))


def inverse_norm(rows):
    return lax.rsqrt(jnp.sum(rows * rows, axis=1, keepdims=True) + EPSILON)


def params():
    return pltpu.CompilerParams(vmem_limit_bytes=VMEM_LIMIT)


def shape(rows, columns=D, dtype=F32):
    return jax.ShapeDtypeStruct((rows, columns), dtype)


def unit_kernel(image_ref, text_ref, image_out, first_out, second_out):
    image = image_ref[...]
    image_out[...] = image * inverse_norm(image)
    text = text_ref[...]
    unit = text * inverse_norm(text)
    first_out[...] = unit[:HALF]
    second_out[...] = unit[HALF:]


def units(image, text):
    return pl.pallas_call(
        unit_kernel,
        out_shape=(shape(ROWS), shape(HALF), shape(HALF)),
        compiler_params=params(),
    )(image, text)


def slopes_kernel(place_ref, scalar_ref, image_hbm, *refs):
    texts = refs[:8]
    direction, slope_high, slope_low = refs[8:11]
    image, text, image_high, image_low, text_high, text_low, sems = refs[11:]
    first = place_ref[0]
    own = place_ref[1]
    image_copy = pltpu.make_async_copy(
        image_hbm.at[pl.ds(pl.multiple_of(first, NEAR), NEAR)], image, sems.at[8]
    )
    image_copy.start()
    copies = []
    for j in range(8):
        copy = pltpu.make_async_copy(texts[j], text.at[pl.ds(j * BUNDLE, BUNDLE)], sems.at[j])
        copy.start()
        copies.append(copy)
    temperature = scalar_ref[0]
    bias = scalar_ref[1]
    image_copy.wait()
    image_high[...], image_low[...] = split(image[...])
    row = lax.broadcasted_iota(jnp.int32, (PAIR, PAIR), 0)
    column = lax.broadcasted_iota(jnp.int32, (PAIR, PAIR), 1)
    for j in range(4):
        copies[2 * j].wait()
        copies[2 * j + 1].wait()
        span = pl.ds(j * PAIR, PAIR)
        text_high[span, :], text_low[span, :] = split(text[span, :])
        for i in range(2):
            rows = pl.ds(i * PAIR, PAIR)
            score = dot3(
                (image_high[rows, :], image_low[rows, :]),
                (text_high[span, :], text_low[span, :]),
                FEATURES,
            )
            score = temperature * score + bias
            if j % 2 == 0:
                own_row = row + (i * PAIR + first - own)
                target = own_row if j == 0 else own_row - HALF
                same = (target == column) & (target >= 0) & (target < HALF)
                score = jnp.where(same, -score, score)
                slope = 1.0 / (1.0 + jnp.exp(-score))
                slope = jnp.where(same, -slope, slope)
            else:
                slope = 1.0 / (1.0 + jnp.exp(-score))
            high, low = split(slope)
            slope_high[rows, span] = high
            slope_low[rows, span] = low
    for i in range(2):
        rows = pl.ds(i * PAIR, PAIR)
        direction[rows, :] = dot3(
            (slope_high[rows, :], slope_low[rows, :]), (text_high[...], text_low[...]), PLAIN
        )


def slopes(place, scalars, image, texts):
    any_space = pl.BlockSpec(memory_space=pl.ANY)
    scalar_space = pl.BlockSpec(memory_space=pltpu.SMEM)
    vector_space = pl.BlockSpec(memory_space=pltpu.VMEM)
    return pl.pallas_call(
        slopes_kernel,
        out_shape=(shape(NEAR), shape(NEAR, SIDE, BF16), shape(NEAR, SIDE, BF16)),
        in_specs=[scalar_space, scalar_space] + [any_space] * 9,
        out_specs=[vector_space] * 3,
        scratch_shapes=[
            pltpu.VMEM((NEAR, D), F32),
            pltpu.VMEM((SIDE, D), F32),
            pltpu.VMEM((NEAR, D), BF16),
            pltpu.VMEM((NEAR, D), BF16),
            pltpu.VMEM((SIDE, D), BF16),
            pltpu.VMEM((SIDE, D), BF16),
            pltpu.SemaphoreType.DMA((9,)),
        ],
        compiler_params=params(),
        cost_estimate=pl.CostEstimate(
            flops=12 * NEAR * SIDE * D, bytes_accessed=16 << 20, transcendentals=2 * NEAR * SIDE
        ),
    )(place, scalars, image, *texts)


def text_kernel(place_ref, image_hbm, *refs):
    slope_refs = refs[:4]
    outs = refs[4:12]
    image, image_high, image_low, sems = refs[12:]
    copies = []
    for k in range(2):
        first = pl.multiple_of(place_ref[k], NEAR)
        copy = pltpu.make_async_copy(
            image_hbm.at[pl.ds(first, NEAR)], image.at[pl.ds(k * NEAR, NEAR)], sems.at[k]
        )
        copy.start()
        copies.append(copy)
    for k in range(2):
        copies[k].wait()
        rows = pl.ds(k * NEAR, NEAR)
        image_high[rows, :], image_low[rows, :] = split(image[rows, :])
    for j in range(4):
        span = pl.ds(j * PAIR, PAIR)
        total = None
        for k in range(2):
            rows = pl.ds(k * NEAR, NEAR)
            part = dot3(
                (slope_refs[2 * k][:, span], slope_refs[2 * k + 1][:, span]),
                (image_high[rows, :], image_low[rows, :]),
                ROWS_ROWS,
            )
            total = part if total is None else total + part
        outs[2 * j][...] = total[:BUNDLE]
        outs[2 * j + 1][...] = total[BUNDLE:]


def text_directions(places, image, slope_parts):
    any_space = pl.BlockSpec(memory_space=pl.ANY)
    scalar_space = pl.BlockSpec(memory_space=pltpu.SMEM)
    vector_space = pl.BlockSpec(memory_space=pltpu.VMEM)
    return pl.pallas_call(
        text_kernel,
        out_shape=(shape(BUNDLE),) * 8,
        in_specs=[scalar_space, any_space] + [vector_space] * 4,
        out_specs=[vector_space] * 8,
        scratch_shapes=[
            pltpu.VMEM((SIDE, D), F32),
            pltpu.VMEM((SIDE, D), BF16),
            pltpu.VMEM((SIDE, D), BF16),
            pltpu.SemaphoreType.DMA((2,)),
        ],
        compiler_params=params(),
        cost_estimate=pl.CostEstimate(
            flops=6 * SIDE * SIDE * D, bytes_accessed=14 << 20, transcendentals=0
        ),
    )(places, image, *slope_parts)


def add_kernel(own, first, second, third, *outs):
    total = (own[...] + first[...]) + (second[...] + third[...])
    for k in range(4):
        outs[k][...] = total[k * HALF : (k + 1) * HALF]


def add_bundles(parts):
    return pl.pallas_call(
        add_kernel, out_shape=(shape(HALF),) * 4, compiler_params=params()
    )(*parts)


def last_kernel(scalar_ref, image_ref, text_ref, image_sum, *refs):
    text_sums = refs[:8]
    image_out, text_out = refs[8:]
    temperature = scalar_ref[0]

    def back_through(rows, direction):
        inverse = inverse_norm(rows)
        unit = rows * inverse
        along = jnp.sum(unit * direction, axis=1, keepdims=True)
        return inverse * (direction - unit * along)

    image_out[...] = back_through(image_ref[...], temperature * image_sum[...])
    for k in range(2):
        a, b, c, d = text_sums[4 * k : 4 * k + 4]
        direction = temperature * ((a[...] + b[...]) + (c[...] + d[...]))
        rows = pl.ds(k * HALF, HALF)
        text_out[rows, :] = back_through(text_ref[rows, :], direction)


def last(scalars, image, text, image_sum, text_sums):
    vector_space = pl.BlockSpec(memory_space=pltpu.VMEM)
    return pl.pallas_call(
        last_kernel,
        out_shape=(shape(ROWS), shape(ROWS)),
        in_specs=[pl.BlockSpec(memory_space=pltpu.SMEM)] + [vector_space] * 11,
        out_specs=[vector_space] * 2,
        compiler_params=params(),
    )(scalars, image, text, image_sum, *text_sums)


def local(image, text, scale_exponent, bias):
    scalars = jnp.concatenate([jnp.exp(scale_exponent), bias])
    core = lax.axis_index("core")
    own = (core * 8 + lax.axis_index("z")) * ROWS
    far_first = (1 - core) * NEAR
    near_first = core * NEAR

    image_unit, first_half, second_half = units(image, text)
    images = lax.all_gather(image_unit, ("core", "z"), axis=0, tiled=True)

    first_x = [first_half] + [shift_x(first_half, by) for by in (1, -1, 2)]
    second_y = [second_half] + [shift_y(second_half, by) for by in (1, -1, 2)]
    first_bundle = jnp.concatenate(first_x, axis=0)
    second_bundle = jnp.concatenate(second_y, axis=0)
    texts = [first_bundle] + [shift_y(first_bundle, by) for by in (1, -1, 2)]
    texts += [second_bundle] + [shift_x(second_bundle, by) for by in (1, -1, 2)]

    def slopes_at(first):
        place = jnp.stack([first, own]).astype(jnp.int32)
        return slopes(place, scalars, images, texts)

    far_direction, far_high, far_low = slopes_at(far_first)
    arrived = swap_core(far_direction)
    near_direction, near_high, near_low = slopes_at(near_first)
    image_sum = lax.psum_scatter(near_direction + arrived, "z", scatter_dimension=0, tiled=True)

    places = jnp.stack([far_first, near_first]).astype(jnp.int32)
    parts = text_directions(places, images, (far_high, far_low, near_high, near_low))
    first_sum = [parts[0]] + [shift_y(parts[k], by) for k, by in ((1, -1), (2, 1), (3, 2))]
    second_sum = [parts[4]] + [shift_x(parts[4 + k], by) for k, by in ((1, -1), (2, 1), (3, 2))]
    first_parts = add_bundles(first_sum)
    second_parts = add_bundles(second_sum)
    text_sums = [first_parts[0]]
    text_sums += [shift_x(first_parts[k], by) for k, by in ((1, -1), (2, 1), (3, 2))]
    text_sums += [second_parts[0]]
    text_sums += [shift_y(second_parts[k], by) for k, by in ((1, -1), (2, 1), (3, 2))]
    return last(scalars, image, text, image_sum, text_sums)


def solution(mesh):
    fine = Mesh(mesh.devices.reshape(2, 8, 2, 4, 2), ("xl", "z", "core", "y", "xh"))
    rows = P(("xl", "z", "core", "y", "xh"), None)
    return jax.shard_map(
        local,
        mesh=fine,
        in_specs=(rows, rows, P(), P()),
        out_specs=(rows, rows),
        check_vma=False,
    )
```

```python
import functools

import jax
import jax.numpy as jnp
from jax import lax
from jax.experimental import pallas as pl
from jax.experimental.pallas import tpu as pltpu
from jax.sharding import Mesh, PartitionSpec as P

EPSILON = 1e-06
D = 1152
ROWS = 64
HALF = 32
BUNDLE = 128
SIDE = 1024
NEAR = 512
PAIR = 256
F32 = jnp.float32
BF16 = jnp.bfloat16
ROWS_ROWS = (((0,), (0,)), ((), ()))
FEATURES = (((1,), (1,)), ((), ()))
PLAIN = (((1,), (0,)), ((), ()))
RING_X = ("xl", "xh")


def x_index(place):
    return (place % 2) * 2 + place // 2


def shift_x(value, by):
    return lax.ppermute(value, RING_X, [(x_index(i), x_index((i + by) % 4)) for i in range(4)])


def shift_y(value, by):
    return lax.ppermute(value, "y", [(i, (i + by) % 4) for i in range(4)])


def swap_core(value):
    return lax.ppermute(value, "core", [(0, 1), (1, 0)])


def split(value):
    high = value.astype(BF16)
    low = (value - high.astype(F32)).astype(BF16)
    return high, low


def dot3(left, right, dims):
    dot = functools.partial(lax.dot_general, dimension_numbers=dims, preferred_element_type=F32)
    return dot(left[0], right[0]) + (dot(left[0], right[1]) + dot(left[1], right[0]))


def inverse_norm(rows):
    return lax.rsqrt(jnp.sum(rows * rows, axis=1, keepdims=True) + EPSILON)


def params(mebibytes):
    return pltpu.CompilerParams(vmem_limit_bytes=mebibytes * 1024 * 1024)


def shape(rows, columns=D, dtype=F32):
    return jax.ShapeDtypeStruct((rows, columns), dtype)


def vmem(rows, columns=D, dtype=F32):
    return pltpu.VMEM((rows, columns), dtype)


def kept(values):
    return [pltpu.with_memory_space_constraint(value, pltpu.VMEM) for value in values]


def outside(values):
    return [pltpu.with_memory_space_constraint(value, pltpu.HBM) for value in values]


ANY_SPACE = pl.BlockSpec(memory_space=pl.ANY)
SCALARS = pl.BlockSpec(memory_space=pltpu.SMEM)
VECTORS = pl.BlockSpec(memory_space=pltpu.VMEM)


def split_units(rows):
    return split(rows * inverse_norm(rows))


def slopes_kernel(scalar_ref, place_ref, image_hbm, *refs):
    texts = refs[:8]
    far_out, text_high_out, text_low_out, image_high, image_low, slope_high, slope_low = refs[8:15]
    image, text_high, text_low, far, sems = refs[15:]
    own = place_ref[1]
    image_copies = []
    for half in range(2):
        first = pl.multiple_of((place_ref[0] + half * NEAR) % SIDE, NEAR)
        copy = pltpu.make_async_copy(
            image_hbm.at[pl.ds(first, NEAR)], image.at[pl.ds(half * NEAR, NEAR)], sems.at[half]
        )
        copy.start()
        image_copies.append(copy)
    copies = []
    temperature = scalar_ref[0]
    bias = scalar_ref[1]
    for pair in range(4):
        span = pl.ds(pair * PAIR, PAIR)
        for k in range(2):
            rows = pl.ds(pair * PAIR + k * BUNDLE, BUNDLE)
            text_high[rows, :], text_low[rows, :] = split_units(texts[4 * k + pair][...])
        for k, (part, out) in enumerate(((text_high, text_high_out), (text_low, text_low_out))):
            copy = pltpu.make_async_copy(part.at[span], out.at[span], sems.at[2 + 2 * pair + k])
            copy.start()
            copies.append(copy)
        for half in range(2):
            rows = pl.ds(half * NEAR, NEAR)
            if pair == 0:
                image_copies[half].wait()
                image_high[rows, :], image_low[rows, :] = split_units(image[rows, :])
            score = dot3(
                (image_high[rows, :], image_low[rows, :]),
                (text_high[span, :], text_low[span, :]),
                FEATURES,
            )
            score = temperature * score + bias
            if pair == 0 and half == 1:
                row = lax.broadcasted_iota(jnp.int32, (NEAR, PAIR), 0) - own
                column = lax.broadcasted_iota(jnp.int32, (NEAR, PAIR), 1)
                target = jnp.where(row < HALF, row, row + (BUNDLE - HALF))
                same = (target == column) & (row >= 0) & (row < ROWS)
                slope = 1.0 / (1.0 + jnp.exp(jnp.where(same, score, -score)))
                slope = jnp.where(same, -slope, slope)
            else:
                slope = 1.0 / (1.0 + jnp.exp(-score))
            slope_high[rows, span], slope_low[rows, span] = split(slope)
    for i in range(2):
        rows = pl.ds(i * PAIR, PAIR)
        far[rows, :] = dot3(
            (slope_high[rows, :], slope_low[rows, :]), (text_high[...], text_low[...]), PLAIN
        )
        copy = pltpu.make_async_copy(far.at[rows], far_out.at[rows], sems.at[10 + i])
        copy.start()
        copies.append(copy)
    for copy in copies:
        copy.wait()


def slopes(scalars, place, image, texts):
    return pl.pallas_call(
        slopes_kernel,
        out_shape=(pltpu.HBM((NEAR, D), F32),)
        + (pltpu.HBM((SIDE, D), BF16),) * 2
        + (vmem(SIDE, D, BF16),) * 2
        + (vmem(SIDE, SIDE, BF16),) * 2,
        in_specs=[SCALARS, SCALARS, ANY_SPACE] + [VECTORS] * 8,
        out_specs=[ANY_SPACE] * 3 + [VECTORS] * 4,
        scratch_shapes=[
            vmem(SIDE),
            vmem(SIDE, D, BF16),
            vmem(SIDE, D, BF16),
            vmem(NEAR),
            pltpu.SemaphoreType.DMA((12,)),
        ],
        compiler_params=params(20),
        cost_estimate=pl.CostEstimate(
            flops=9 * SIDE * SIDE * D, bytes_accessed=10 << 20, transcendentals=2 * SIDE * SIDE
        ),
    )(scalars, place, *outside([image]), *kept(texts))


def near_kernel(arrived, text_high_hbm, text_low_hbm, slope_high, slope_low, out, *scratch):
    text_high, text_low, total, sems = scratch
    fetched = []
    for k, (part, place) in enumerate(((text_high_hbm, text_high), (text_low_hbm, text_low))):
        copy = pltpu.make_async_copy(part, place, sems.at[k])
        copy.start()
        fetched.append(copy)
    for copy in fetched:
        copy.wait()
    copies = []
    for i in range(2):
        rows = pl.ds(i * PAIR, PAIR)
        near = pl.ds(NEAR + i * PAIR, PAIR)
        direction = dot3(
            (slope_high[near, :], slope_low[near, :]), (text_high[...], text_low[...]), PLAIN
        )
        total[rows, :] = arrived[rows, :] + direction
        copy = pltpu.make_async_copy(total.at[rows], out.at[rows], sems.at[2 + i])
        copy.start()
        copies.append(copy)
    for copy in copies:
        copy.wait()


def near_directions(arrived, slope_parts, text_parts):
    return pl.pallas_call(
        near_kernel,
        out_shape=pltpu.HBM((NEAR, D), F32),
        in_specs=[VECTORS] + [ANY_SPACE] * 2 + [VECTORS] * 2,
        out_specs=ANY_SPACE,
        scratch_shapes=[vmem(SIDE, D, BF16)] * 2
        + [vmem(NEAR), pltpu.SemaphoreType.DMA((4,))],
        compiler_params=params(13),
        cost_estimate=pl.CostEstimate(
            flops=3 * SIDE * SIDE * D, bytes_accessed=10 << 20, transcendentals=0
        ),
    )(*kept([arrived]), *outside(text_parts), *kept(slope_parts))


def text_kernel(slope_high, slope_low, image_high, image_low, *outs):
    for pair in range(4):
        span = pl.ds(pair * PAIR, PAIR)
        total = dot3(
            (slope_high[:, span], slope_low[:, span]), (image_high[...], image_low[...]), ROWS_ROWS
        )
        outs[pair][...] = total[:BUNDLE]
        outs[4 + pair][...] = total[BUNDLE:]


def text_directions(slope_parts, image_parts):
    return pl.pallas_call(
        text_kernel,
        out_shape=(vmem(BUNDLE),) * 8,
        in_specs=[VECTORS] * 4,
        out_specs=[VECTORS] * 8,
        compiler_params=params(9),
        cost_estimate=pl.CostEstimate(
            flops=6 * SIDE * SIDE * D, bytes_accessed=1 << 20, transcendentals=0
        ),
    )(*kept([*slope_parts, *image_parts]))


def add_kernel(own, first, second, third, *outs):
    for k in range(4):
        rows = pl.ds(k * HALF, HALF)
        outs[k][...] = (own[rows, :] + first[rows, :]) + (second[rows, :] + third[rows, :])


def add_bundles(parts):
    return pl.pallas_call(
        add_kernel,
        out_shape=(vmem(HALF),) * 4,
        in_specs=[VECTORS] * 4,
        out_specs=[VECTORS] * 4,
        compiler_params=params(4),
    )(*kept(parts))


def last_kernel(scalar_ref, image_ref, text_ref, image_sum, *refs):
    text_sums = refs[:8]
    image_out, text_out = refs[8:]
    temperature = scalar_ref[0]

    def back_through(rows, direction):
        inverse = inverse_norm(rows)
        unit = rows * inverse
        along = jnp.sum(unit * direction, axis=1, keepdims=True)
        return inverse * (direction - unit * along)

    image_out[...] = back_through(image_ref[...], temperature * image_sum[...])
    for k in range(2):
        a, b, c, d = text_sums[4 * k : 4 * k + 4]
        direction = temperature * ((a[...] + b[...]) + (c[...] + d[...]))
        rows = pl.ds(k * HALF, HALF)
        text_out[rows, :] = back_through(text_ref[rows, :], direction)


def last(scalars, image, text, image_sum, text_sums):
    return pl.pallas_call(
        last_kernel,
        out_shape=(shape(ROWS), shape(ROWS)),
        in_specs=[SCALARS] + [VECTORS] * 11,
        out_specs=[VECTORS] * 2,
        compiler_params=params(4),
    )(scalars, image, text, image_sum, *kept(text_sums))


def exchange(x_values, y_values):
    steps = (1, -1, 2)
    from_x = [shift_x(value, by) for value, by in zip(x_values, steps)]
    from_y = [shift_y(value, by) for value, by in zip(y_values, steps)]
    return from_x, from_y


def local(image, text, scale_exponent, bias):
    scalars = jnp.concatenate([jnp.exp(scale_exponent), bias])
    core = lax.axis_index("core")
    place = jnp.stack([(1 - core) * NEAR, lax.axis_index("z") * ROWS]).astype(jnp.int32)

    images = lax.all_gather(image, ("core", "z"), axis=0, tiled=True)

    first_half, second_half = text[:HALF], text[HALF:]
    from_x, from_y = exchange([first_half] * 3, [second_half] * 3)
    first_bundle = jnp.concatenate([first_half] + from_x, axis=0)
    second_bundle = jnp.concatenate([second_half] + from_y, axis=0)
    first_bundle, second_bundle = lax.optimization_barrier((first_bundle, second_bundle))
    from_x, from_y = exchange([second_bundle] * 3, [first_bundle] * 3)
    texts = [first_bundle] + from_y + [second_bundle] + from_x

    far, *parts = slopes(scalars, place, images, texts)
    text_parts, image_parts, slope_parts = parts[:2], parts[2:4], parts[4:]
    arrived = swap_core(far)
    sums = text_directions(slope_parts, image_parts)
    arrived, sums = lax.optimization_barrier((arrived, sums))
    near = near_directions(arrived, slope_parts, text_parts)
    image_sum = lax.psum_scatter(near, "z", scatter_dimension=0, tiled=True)

    from_x, from_y = exchange([sums[6], sums[5], sums[7]], [sums[2], sums[1], sums[3]])
    first_parts = add_bundles([sums[0]] + from_y)
    second_parts = add_bundles([sums[4]] + from_x)
    from_x, from_y = exchange(
        [first_parts[2], first_parts[1], first_parts[3]],
        [second_parts[2], second_parts[1], second_parts[3]],
    )
    text_sums = [first_parts[0]] + from_x + [second_parts[0]] + from_y
    return last(scalars, image, text, image_sum, text_sums)


def solution(mesh):
    fine = Mesh(mesh.devices.reshape(2, 8, 2, 4, 2), ("xl", "z", "core", "y", "xh"))
    rows = P(("xl", "z", "core", "y", "xh"), None)
    return jax.shard_map(
        local,
        mesh=fine,
        in_specs=(rows, rows, P(), P()),
        out_specs=(rows, rows),
        check_vma=False,
    )
```

```python
import functools

import jax
import jax.numpy as jnp
from jax import lax
from jax.experimental import pallas as pl
from jax.experimental.pallas import tpu as pltpu
from jax.sharding import Mesh, PartitionSpec as P

EPSILON = 1e-06
D = 1152
ROWS = 64
HALF = 32
BUNDLE = 128
SIDE = 1024
NEAR = 512
PAIR = 256
F32 = jnp.float32
BF16 = jnp.bfloat16
ROWS_ROWS = (((0,), (0,)), ((), ()))
FEATURES = (((1,), (1,)), ((), ()))
PLAIN = (((1,), (0,)), ((), ()))
RING_X = ("xl", "xh")


def x_index(place):
    return (place % 2) * 2 + place // 2


def shift_x(value, by):
    return lax.ppermute(value, RING_X, [(x_index(i), x_index((i + by) % 4)) for i in range(4)])


def shift_y(value, by):
    return lax.ppermute(value, "y", [(i, (i + by) % 4) for i in range(4)])


def swap_core(value):
    return lax.ppermute(value, "core", [(0, 1), (1, 0)])


def split(value):
    high = value.astype(BF16)
    low = (value - high.astype(F32)).astype(BF16)
    return high, low


def dot3(left, right, dims):
    dot = functools.partial(lax.dot_general, dimension_numbers=dims, preferred_element_type=F32)
    return dot(left[0], right[0]) + (dot(left[0], right[1]) + dot(left[1], right[0]))


def inverse_norm(rows):
    return lax.rsqrt(jnp.sum(rows * rows, axis=1, keepdims=True) + EPSILON)


def params(mebibytes):
    return pltpu.CompilerParams(vmem_limit_bytes=mebibytes * 1024 * 1024)


def shape(rows, columns=D, dtype=F32):
    return jax.ShapeDtypeStruct((rows, columns), dtype)


def vmem(rows, columns=D, dtype=F32):
    return pltpu.VMEM((rows, columns), dtype)


def kept(values):
    return [pltpu.with_memory_space_constraint(value, pltpu.VMEM) for value in values]


def outside(values):
    return [pltpu.with_memory_space_constraint(value, pltpu.HBM) for value in values]


ANY_SPACE = pl.BlockSpec(memory_space=pl.ANY)
SCALARS = pl.BlockSpec(memory_space=pltpu.SMEM)
VECTORS = pl.BlockSpec(memory_space=pltpu.VMEM)


BRIEF = pl.CostEstimate(flops=SIDE, bytes_accessed=SIDE, transcendentals=0)


def split_units(rows):
    return split(rows * inverse_norm(rows))


def slopes_kernel(scalar_ref, place_ref, image_hbm, *refs):
    texts = refs[:8]
    far_out, text_high_out, text_low_out, image_high, image_low, slope_high, slope_low = refs[8:15]
    near, far, text, text_high, text_low, sems = refs[15:]
    own = place_ref[1]
    image_copies = []
    text_copies = []

    def fetch_image(half):
        first = pl.multiple_of((place_ref[0] + half * NEAR) % SIDE, NEAR)
        copy = pltpu.make_async_copy(
            image_hbm.at[pl.ds(first, NEAR)], (far, near)[half], sems.at[half]
        )
        copy.start()
        image_copies.append(copy)

    def fetch_text(pair):
        for k in range(2):
            copy = pltpu.make_async_copy(
                texts[2 * pair + k],
                text.at[pl.ds(pair % 2 * PAIR + k * BUNDLE, BUNDLE)],
                sems.at[2 + 2 * pair + k],
            )
            copy.start()
            text_copies.append(copy)

    fetch_text(0)
    fetch_image(0)
    fetch_image(1)
    fetch_text(1)
    temperature = scalar_ref[0]
    bias = scalar_ref[1]
    for pair in range(4):
        span = pl.ds(pair * PAIR, PAIR)
        text_copies[2 * pair].wait()
        text_copies[2 * pair + 1].wait()
        staged = pl.ds(pair % 2 * PAIR, PAIR)
        text_high[span, :], text_low[span, :] = split_units(text[staged, :])
        if pair < 2:
            fetch_text(pair + 2)
        for half in range(2):
            rows = pl.ds(half * NEAR, NEAR)
            if pair == 0:
                image_copies[half].wait()
                image_high[rows, :], image_low[rows, :] = split_units((far, near)[half][...])
            score = dot3(
                (image_high[rows, :], image_low[rows, :]),
                (text_high[span, :], text_low[span, :]),
                FEATURES,
            )
            score = temperature * score + bias
            if pair % 2 == 0 and half == 1:
                row = lax.broadcasted_iota(jnp.int32, (NEAR, PAIR), 0) - (own + pair // 2 * HALF)
                column = lax.broadcasted_iota(jnp.int32, (NEAR, PAIR), 1)
                same = (row == column) & (row >= 0) & (row < HALF)
                slope = 1.0 / (1.0 + jnp.exp(jnp.where(same, score, -score)))
                slope = jnp.where(same, -slope, slope)
            else:
                slope = 1.0 / (1.0 + jnp.exp(-score))
            slope_high[rows, span], slope_low[rows, span] = split(slope)
    copies = []
    for k, (part, out) in enumerate(((text_high, text_high_out), (text_low, text_low_out))):
        copy = pltpu.make_async_copy(part, out, sems.at[10 + k])
        copy.start()
        copies.append(copy)
    for i in range(2):
        rows = pl.ds(i * PAIR, PAIR)
        far[rows, :] = dot3(
            (slope_high[rows, :], slope_low[rows, :]), (text_high[...], text_low[...]), PLAIN
        )
        copy = pltpu.make_async_copy(far.at[rows], far_out.at[rows], sems.at[12 + i])
        copy.start()
        copies.append(copy)
    for copy in copies:
        copy.wait()


def slopes(scalars, place, image, texts):
    return pl.pallas_call(
        slopes_kernel,
        out_shape=(pltpu.HBM((NEAR, D), F32),)
        + (pltpu.HBM((SIDE, D), BF16),) * 2
        + (vmem(SIDE, D, BF16),) * 2
        + (vmem(SIDE, SIDE, BF16),) * 2,
        in_specs=[SCALARS, SCALARS] + [ANY_SPACE] * 9,
        out_specs=[ANY_SPACE] * 3 + [VECTORS] * 4,
        scratch_shapes=[vmem(NEAR), vmem(NEAR), vmem(2 * PAIR)]
        + [vmem(SIDE, D, BF16)] * 2
        + [pltpu.SemaphoreType.DMA((14,))],
        compiler_params=params(20),
        cost_estimate=pl.CostEstimate(
            flops=9 * SIDE * SIDE * D, bytes_accessed=10 << 20, transcendentals=2 * SIDE * SIDE
        ),
    )(scalars, place, *outside([image, *texts]))


def near_kernel(arrived, text_high_hbm, text_low_hbm, slope_high, slope_low, out, *scratch):
    text_high, text_low, total, sems = scratch
    copies = []
    for k, (part, place) in enumerate(((text_high_hbm, text_high), (text_low_hbm, text_low))):
        copy = pltpu.make_async_copy(part, place, sems.at[k])
        copy.start()
        copies.append(copy)
    near = pl.ds(NEAR, NEAR)
    dot = functools.partial(lax.dot_general, dimension_numbers=PLAIN, preferred_element_type=F32)
    copies[0].wait()
    total[...] = arrived[...] + (
        dot(slope_high[near, :], text_high[...]) + dot(slope_low[near, :], text_high[...])
    )
    copies[1].wait()
    copies = []
    for i in range(2):
        rows = pl.ds(i * PAIR, PAIR)
        near = pl.ds(NEAR + i * PAIR, PAIR)
        total[rows, :] += dot(slope_high[near, :], text_low[...])
        copy = pltpu.make_async_copy(total.at[rows], out.at[rows], sems.at[2 + i])
        copy.start()
        copies.append(copy)
    for copy in copies:
        copy.wait()


def near_directions(arrived, slope_parts, text_parts):
    return pl.pallas_call(
        near_kernel,
        out_shape=pltpu.HBM((NEAR, D), F32),
        in_specs=[VECTORS] + [ANY_SPACE] * 2 + [VECTORS] * 2,
        out_specs=ANY_SPACE,
        scratch_shapes=[vmem(SIDE, D, BF16)] * 2 + [vmem(NEAR), pltpu.SemaphoreType.DMA((4,))],
        compiler_params=params(20),
        cost_estimate=BRIEF,
    )(*kept([arrived]), *outside(text_parts), *kept(slope_parts))


def text_kernel(slope_high, slope_low, image_high, image_low, *refs):
    outs = refs[:8]
    total, sems = refs[8:]
    copies = []
    for pair in range(4):
        span = pl.ds(pair * PAIR, PAIR)
        total[span, :] = dot3(
            (slope_high[:, span], slope_low[:, span]), (image_high[...], image_low[...]), ROWS_ROWS
        )
        for k in (2 * pair, 2 * pair + 1):
            copy = pltpu.make_async_copy(total.at[pl.ds(k * BUNDLE, BUNDLE)], outs[k], sems.at[k])
            copy.start()
            copies.append(copy)
    for copy in copies:
        copy.wait()


def text_directions(slope_parts, image_parts):
    return pl.pallas_call(
        text_kernel,
        out_shape=(pltpu.HBM((BUNDLE, D), F32),) * 8,
        in_specs=[VECTORS] * 4,
        out_specs=[ANY_SPACE] * 8,
        scratch_shapes=[vmem(SIDE), pltpu.SemaphoreType.DMA((8,))],
        compiler_params=params(14),
        cost_estimate=BRIEF,
    )(*kept([*slope_parts, *image_parts]))


def add_kernel(own, first, second, third, *outs):
    for k in range(4):
        rows = pl.ds(k * HALF, HALF)
        outs[k][...] = (own[rows, :] + first[rows, :]) + (second[rows, :] + third[rows, :])


def add_bundles(parts):
    return pl.pallas_call(
        add_kernel,
        out_shape=(vmem(HALF),) * 4,
        in_specs=[VECTORS] * 4,
        out_specs=[VECTORS] * 4,
        compiler_params=params(4),
    )(*kept(parts))


def last_kernel(scalar_ref, image_ref, text_ref, image_sum, *refs):
    text_sums = refs[:8]
    image_out, text_out = refs[8:]
    temperature = scalar_ref[0]

    def back_through(rows, direction):
        inverse = inverse_norm(rows)
        unit = rows * inverse
        along = jnp.sum(unit * direction, axis=1, keepdims=True)
        return inverse * (direction - unit * along)

    image_out[...] = back_through(image_ref[...], temperature * image_sum[...])
    for k in range(2):
        a, b, c, d = text_sums[4 * k : 4 * k + 4]
        direction = temperature * ((a[...] + b[...]) + (c[...] + d[...]))
        rows = pl.ds(k * HALF, HALF)
        text_out[rows, :] = back_through(text_ref[rows, :], direction)


def last(scalars, image, text, image_sum, text_sums):
    return pl.pallas_call(
        last_kernel,
        out_shape=(shape(ROWS), shape(ROWS)),
        in_specs=[SCALARS] + [VECTORS] * 11,
        out_specs=[VECTORS] * 2,
        compiler_params=params(4),
    )(scalars, image, text, image_sum, *kept(text_sums))


def around(shift, values):
    return [shift(value, by) for value, by in zip(values, (1, -1, 2))]


def back_around(shift, values):
    return around(shift, [values[2], values[1], values[3]])


def local(image, text, scale_exponent, bias):
    scalars = jnp.concatenate([jnp.exp(scale_exponent), bias])
    core = lax.axis_index("core")
    place = jnp.stack([(1 - core) * NEAR, lax.axis_index("z") * ROWS]).astype(jnp.int32)

    images = lax.all_gather(image, ("core", "z"), axis=0, tiled=True)

    first_half, second_half = text[:HALF], text[HALF:]
    first_bundle = jnp.concatenate([first_half] + around(shift_x, [first_half] * 3), axis=0)
    second_bundle = jnp.concatenate([second_half] + around(shift_y, [second_half] * 3), axis=0)
    first_bundle, second_bundle = lax.optimization_barrier((first_bundle, second_bundle))
    texts = [first_bundle] + around(shift_y, [first_bundle] * 3)
    texts += [second_bundle] + around(shift_x, [second_bundle] * 3)

    far, *parts = slopes(scalars, place, images, texts)
    text_parts, image_parts, slope_parts = parts[:2], parts[2:4], parts[4:]
    arrived = swap_core(far)
    sums = text_directions(slope_parts, image_parts)
    arrived, sums = lax.optimization_barrier((arrived, sums))
    first_sums, second_sums = sums[:4], sums[4:]
    near = near_directions(arrived, slope_parts, text_parts)
    image_sum = lax.psum_scatter(near, "z", scatter_dimension=0, tiled=True)
    first_sent = back_around(shift_y, first_sums)
    second_sent = back_around(shift_x, second_sums)
    first_parts = add_bundles([first_sums[0]] + first_sent)
    text_sums = [first_parts[0]] + back_around(shift_x, first_parts)
    second_parts = add_bundles([second_sums[0]] + second_sent)
    text_sums += [second_parts[0]] + back_around(shift_y, second_parts)
    return last(scalars, image, text, image_sum, text_sums)


def solution(mesh):
    fine = Mesh(mesh.devices.reshape(2, 8, 2, 4, 2), ("xl", "z", "core", "y", "xh"))
    rows = P(("xl", "z", "core", "y", "xh"), None)
    return jax.shard_map(
        local,
        mesh=fine,
        in_specs=(rows, rows, P(), P()),
        out_specs=(rows, rows),
        check_vma=False,
    )
```

```python
import functools

import jax
import jax.numpy as jnp
from jax import lax
from jax.experimental import pallas as pl
from jax.experimental.pallas import tpu as pltpu
from jax.sharding import Mesh, PartitionSpec as P

EPSILON = 1e-06
D = 1152
ROWS = 64
HALF = 32
BUNDLE = 128
SIDE = 1024
NEAR = 512
PAIR = 256
F32 = jnp.float32
BF16 = jnp.bfloat16
ROWS_ROWS = (((0,), (0,)), ((), ()))
FEATURES = (((1,), (1,)), ((), ()))
PLAIN = (((1,), (0,)), ((), ()))
RING_X = ("xl", "xh")


def x_index(place):
    return (place % 2) * 2 + place // 2


def shift_x(value, by):
    return lax.ppermute(value, RING_X, [(x_index(i), x_index((i + by) % 4)) for i in range(4)])


def shift_y(value, by):
    return lax.ppermute(value, "y", [(i, (i + by) % 4) for i in range(4)])


def swap_core(value):
    return lax.ppermute(value, "core", [(0, 1), (1, 0)])


def split(value):
    high = value.astype(BF16)
    low = (value - high.astype(F32)).astype(BF16)
    return high, low


def dot3(left, right, dims):
    dot = functools.partial(lax.dot_general, dimension_numbers=dims, preferred_element_type=F32)
    return dot(left[0], right[0]) + (dot(left[0], right[1]) + dot(left[1], right[0]))


def inverse_norm(rows):
    return lax.rsqrt(jnp.sum(rows * rows, axis=1, keepdims=True) + EPSILON)


def params(mebibytes):
    return pltpu.CompilerParams(vmem_limit_bytes=mebibytes * 1024 * 1024)


def shape(rows, columns=D, dtype=F32):
    return jax.ShapeDtypeStruct((rows, columns), dtype)


def vmem(rows, columns=D, dtype=F32):
    return pltpu.VMEM((rows, columns), dtype)


def kept(values):
    return [pltpu.with_memory_space_constraint(value, pltpu.VMEM) for value in values]


def outside(values):
    return [pltpu.with_memory_space_constraint(value, pltpu.HBM) for value in values]


ANY_SPACE = pl.BlockSpec(memory_space=pl.ANY)
SCALARS = pl.BlockSpec(memory_space=pltpu.SMEM)
VECTORS = pl.BlockSpec(memory_space=pltpu.VMEM)


BRIEF = pl.CostEstimate(flops=SIDE, bytes_accessed=SIDE, transcendentals=0)


def split_units(rows):
    return split(rows * inverse_norm(rows))


def slopes_kernel(scalar_ref, place_ref, image_hbm, *refs):
    texts = refs[:8]
    far_out, text_high, text_low, image_high, image_low, slope_high, slope_low = refs[8:15]
    image, far, sems = refs[15:]
    own = place_ref[1]
    image_copies = []
    for chunk in range(4):
        first = pl.multiple_of((place_ref[0] + chunk * PAIR) % SIDE, PAIR)
        copy = pltpu.make_async_copy(
            image_hbm.at[pl.ds(first, PAIR)], image.at[pl.ds(chunk * PAIR, PAIR)], sems.at[chunk]
        )
        copy.start()
        image_copies.append(copy)
    temperature = scalar_ref[0]
    bias = scalar_ref[1]
    for k in range(8):
        rows = pl.ds(k * BUNDLE, BUNDLE)
        text_high[rows, :], text_low[rows, :] = split_units(texts[k][...])
    for chunk in range(4):
        rows = pl.ds(chunk * PAIR, PAIR)
        image_copies[chunk].wait()
        image_high[rows, :], image_low[rows, :] = split_units(image[rows, :])
        for pair in range(4):
            span = pl.ds(pair * PAIR, PAIR)
            score = dot3(
                (image_high[rows, :], image_low[rows, :]),
                (text_high[span, :], text_low[span, :]),
                FEATURES,
            )
            score = temperature * score + bias
            if pair % 2 == 0 and chunk >= 2:
                start = own + pair // 2 * HALF - (chunk - 2) * PAIR
                row = lax.broadcasted_iota(jnp.int32, (PAIR, PAIR), 0) - start
                column = lax.broadcasted_iota(jnp.int32, (PAIR, PAIR), 1)
                same = (row == column) & (row >= 0) & (row < HALF)
                slope = 1.0 / (1.0 + jnp.exp(jnp.where(same, score, -score)))
                slope = jnp.where(same, -slope, slope)
            else:
                slope = 1.0 / (1.0 + jnp.exp(-score))
            slope_high[rows, span], slope_low[rows, span] = split(slope)
    copies = []
    for i in range(2):
        rows = pl.ds(i * PAIR, PAIR)
        far[rows, :] = dot3(
            (slope_high[rows, :], slope_low[rows, :]), (text_high[...], text_low[...]), PLAIN
        )
        copy = pltpu.make_async_copy(far.at[rows], far_out.at[rows], sems.at[6 + i])
        copy.start()
        copies.append(copy)
    for copy in copies:
        copy.wait()


def slopes(scalars, place, image, texts):
    return pl.pallas_call(
        slopes_kernel,
        out_shape=(pltpu.HBM((NEAR, D), F32),)
        + (vmem(SIDE, D, BF16),) * 4
        + (vmem(SIDE, SIDE, BF16),) * 2,
        in_specs=[SCALARS, SCALARS, ANY_SPACE] + [VECTORS] * 8,
        out_specs=[ANY_SPACE] + [VECTORS] * 6,
        scratch_shapes=[
            vmem(SIDE),
            vmem(NEAR),
            pltpu.SemaphoreType.DMA((8,)),
        ],
        compiler_params=params(20),
        cost_estimate=pl.CostEstimate(
            flops=9 * SIDE * SIDE * D, bytes_accessed=10 << 20, transcendentals=2 * SIDE * SIDE
        ),
    )(scalars, place, *outside([image]), *kept(texts))


def near_kernel(arrived, text_high, text_low, slope_high, slope_low, out, total, sems):
    copies = []
    for i in range(2):
        rows = pl.ds(i * PAIR, PAIR)
        near = pl.ds(NEAR + i * PAIR, PAIR)
        direction = dot3(
            (slope_high[near, :], slope_low[near, :]), (text_high[...], text_low[...]), PLAIN
        )
        total[rows, :] = arrived[rows, :] + direction
        copy = pltpu.make_async_copy(total.at[rows], out.at[rows], sems.at[i])
        copy.start()
        copies.append(copy)
    for copy in copies:
        copy.wait()


def near_directions(arrived, slope_parts, text_parts):
    return pl.pallas_call(
        near_kernel,
        out_shape=pltpu.HBM((NEAR, D), F32),
        in_specs=[VECTORS] * 5,
        out_specs=ANY_SPACE,
        scratch_shapes=[vmem(NEAR), pltpu.SemaphoreType.DMA((2,))],
        compiler_params=params(12),
        cost_estimate=BRIEF,
    )(*kept([arrived, *text_parts, *slope_parts]))


def text_kernel(slope_high, slope_low, image_high, image_low, *refs):
    outs = refs[:8]
    total, sems = refs[8:]
    copies = []
    for pair in range(4):
        span = pl.ds(pair * PAIR, PAIR)
        total[span, :] = dot3(
            (slope_high[:, span], slope_low[:, span]), (image_high[...], image_low[...]), ROWS_ROWS
        )
        for k in (2 * pair, 2 * pair + 1):
            copy = pltpu.make_async_copy(total.at[pl.ds(k * BUNDLE, BUNDLE)], outs[k], sems.at[k])
            copy.start()
            copies.append(copy)
    for copy in copies:
        copy.wait()


def text_directions(slope_parts, image_parts):
    return pl.pallas_call(
        text_kernel,
        out_shape=(pltpu.HBM((BUNDLE, D), F32),) * 8,
        in_specs=[VECTORS] * 4,
        out_specs=[ANY_SPACE] * 8,
        scratch_shapes=[vmem(SIDE), pltpu.SemaphoreType.DMA((8,))],
        compiler_params=params(14),
        cost_estimate=BRIEF,
    )(*kept([*slope_parts, *image_parts]))


def add_kernel(own, first, second, third, *outs):
    for k in range(4):
        rows = pl.ds(k * HALF, HALF)
        outs[k][...] = (own[rows, :] + first[rows, :]) + (second[rows, :] + third[rows, :])


def add_bundles(parts):
    return pl.pallas_call(
        add_kernel,
        out_shape=(vmem(HALF),) * 4,
        in_specs=[VECTORS] * 4,
        out_specs=[VECTORS] * 4,
        compiler_params=params(4),
    )(*kept(parts))


def last_kernel(scalar_ref, image_ref, text_ref, image_sum, *refs):
    text_sums = refs[:8]
    image_out, text_out = refs[8:]
    temperature = scalar_ref[0]

    def back_through(rows, direction):
        inverse = inverse_norm(rows)
        unit = rows * inverse
        along = jnp.sum(unit * direction, axis=1, keepdims=True)
        return inverse * (direction - unit * along)

    image_out[...] = back_through(image_ref[...], temperature * image_sum[...])
    for k in range(2):
        a, b, c, d = text_sums[4 * k : 4 * k + 4]
        direction = temperature * ((a[...] + b[...]) + (c[...] + d[...]))
        rows = pl.ds((1 - k) * HALF, HALF)
        text_out[rows, :] = back_through(text_ref[rows, :], direction)


def last(scalars, image, text, image_sum, text_sums):
    return pl.pallas_call(
        last_kernel,
        out_shape=(shape(ROWS), shape(ROWS)),
        in_specs=[SCALARS] + [VECTORS] * 11,
        out_specs=[VECTORS] * 2,
        compiler_params=params(4),
    )(scalars, image, text, image_sum, *kept(text_sums))


def around(shift, values):
    return [shift(value, by) for value, by in zip(values, (1, -1, 2))]


def send_back(y_values, x_values):
    from_y = [shift_y(y_values[2], 1), shift_y(y_values[1], -1)]
    from_x = [shift_x(x_values[2], 1), shift_x(x_values[1], -1)]
    from_y.append(shift_y(y_values[3], 2))
    from_x.append(shift_x(x_values[3], 2))
    return from_y, from_x


def local(image, text, scale_exponent, bias):
    scalars = jnp.concatenate([jnp.exp(scale_exponent), bias])
    core = lax.axis_index("core")
    place = jnp.stack([(1 - core) * NEAR, lax.axis_index("z") * ROWS]).astype(jnp.int32)

    images = lax.all_gather(image, ("core", "z"), axis=0, tiled=True)

    first_half, second_half = text[:HALF], text[HALF:]
    first_bundle = jnp.concatenate([first_half] + around(shift_x, [first_half] * 3), axis=0)
    second_bundle = jnp.concatenate([second_half] + around(shift_y, [second_half] * 3), axis=0)
    first_bundle, second_bundle = lax.optimization_barrier((first_bundle, second_bundle))
    texts = [first_bundle] + around(shift_y, [first_bundle] * 3)
    texts += [second_bundle] + around(shift_x, [second_bundle] * 3)

    far, *parts = slopes(scalars, place, images, texts)
    text_parts, image_parts, slope_parts = parts[:2], parts[2:4], parts[4:]
    arrived = swap_core(far)
    sums = text_directions(slope_parts, image_parts)
    arrived, sums = lax.optimization_barrier((arrived, sums))
    first_sums, second_sums = sums[:4], sums[4:]
    near = near_directions(arrived, slope_parts, text_parts)
    image_sum = lax.psum_scatter(near, "z", scatter_dimension=0, tiled=True)
    first_sent, second_sent = send_back(first_sums, second_sums)
    first_parts = add_bundles([first_sums[0]] + first_sent)
    second_parts = add_bundles([second_sums[0]] + second_sent)
    second_sent, first_sent = send_back(second_parts, first_parts)
    text_sums = [second_parts[0]] + second_sent + [first_parts[0]] + first_sent
    return last(scalars, image, text, image_sum, text_sums)


def solution(mesh):
    fine = Mesh(mesh.devices.reshape(2, 8, 2, 4, 2), ("xl", "z", "core", "y", "xh"))
    rows = P(("xl", "z", "core", "y", "xh"), None)
    return jax.shard_map(
        local,
        mesh=fine,
        in_specs=(rows, rows, P(), P()),
        out_specs=(rows, rows),
        check_vma=False,
    )
```

```python
import functools

import jax
import jax.numpy as jnp
from jax import lax
from jax.experimental import pallas as pl
from jax.experimental.pallas import tpu as pltpu
from jax.sharding import Mesh, PartitionSpec as P

EPSILON = 1e-06
D = 1152
ROWS = 64
HALF = 32
BUNDLE = 128
SIDE = 1024
NEAR = 512
PAIR = 256
F32 = jnp.float32
BF16 = jnp.bfloat16
ROWS_ROWS = (((0,), (0,)), ((), ()))
FEATURES = (((1,), (1,)), ((), ()))
PLAIN = (((1,), (0,)), ((), ()))
EARLY = (0, 1, 2, 3, 4)
LATE = (5, 6, 7)
RING_X = ("xl", "xh")


def x_index(place):
    return (place % 2) * 2 + place // 2


def shift_x(value, by):
    return lax.ppermute(value, RING_X, [(x_index(i), x_index((i + by) % 4)) for i in range(4)])


def shift_y(value, by):
    return lax.ppermute(value, "y", [(i, (i + by) % 4) for i in range(4)])


def swap_core(value):
    return lax.ppermute(value, "core", [(0, 1), (1, 0)])


def split(value):
    high = value.astype(BF16)
    low = (value - high.astype(F32)).astype(BF16)
    return high, low


def dot3(left, right, dims):
    dot = functools.partial(lax.dot_general, dimension_numbers=dims, preferred_element_type=F32)
    return dot(left[0], right[0]) + (dot(left[0], right[1]) + dot(left[1], right[0]))


def inverse_norm(rows):
    return lax.rsqrt(jnp.sum(rows * rows, axis=1, keepdims=True) + EPSILON)


def params(mebibytes):
    return pltpu.CompilerParams(vmem_limit_bytes=mebibytes * 1024 * 1024)


def shape(rows, columns=D, dtype=F32):
    return jax.ShapeDtypeStruct((rows, columns), dtype)


def vmem(rows, columns=D, dtype=F32):
    return pltpu.VMEM((rows, columns), dtype)


def kept(values):
    return [pltpu.with_memory_space_constraint(value, pltpu.VMEM) for value in values]


def outside(values):
    return [pltpu.with_memory_space_constraint(value, pltpu.HBM) for value in values]


ANY_SPACE = pl.BlockSpec(memory_space=pl.ANY)
SCALARS = pl.BlockSpec(memory_space=pltpu.SMEM)
VECTORS = pl.BlockSpec(memory_space=pltpu.VMEM)


BRIEF = pl.CostEstimate(flops=SIDE, bytes_accessed=SIDE, transcendentals=0)


def split_units(rows):
    return split(rows * inverse_norm(rows))


def slopes_kernel(scalar_ref, place_ref, image_hbm, *refs):
    texts = refs[:8]
    far_out, text_high, text_low, image_high, image_low, slope_high, slope_low = refs[8:15]
    image, late, far, sems = refs[15:]
    own = place_ref[1]
    late_copies = []
    for k in range(len(LATE)):
        copy = pltpu.make_async_copy(
            texts[LATE[k]], late.at[pl.ds(k * BUNDLE, BUNDLE)], sems.at[8 + k]
        )
        copy.start()
        late_copies.append(copy)
    image_copies = []
    for chunk in range(4):
        first = pl.multiple_of((place_ref[0] + chunk * PAIR) % SIDE, PAIR)
        copy = pltpu.make_async_copy(
            image_hbm.at[pl.ds(first, PAIR)], image.at[pl.ds(chunk * PAIR, PAIR)], sems.at[chunk]
        )
        copy.start()
        image_copies.append(copy)
    temperature = scalar_ref[0]
    bias = scalar_ref[1]
    for bundle in EARLY:
        rows = pl.ds(bundle * BUNDLE, BUNDLE)
        text_high[rows, :], text_low[rows, :] = split_units(texts[bundle][...])
    for copy in late_copies:
        copy.wait()
    for k, bundle in enumerate(LATE):
        rows = pl.ds(bundle * BUNDLE, BUNDLE)
        text_high[rows, :], text_low[rows, :] = split_units(late[pl.ds(k * BUNDLE, BUNDLE), :])
    for chunk in range(4):
        rows = pl.ds(chunk * PAIR, PAIR)
        image_copies[chunk].wait()
        image_high[rows, :], image_low[rows, :] = split_units(image[rows, :])
        for pair in range(4):
            span = pl.ds(pair * PAIR, PAIR)
            score = dot3(
                (image_high[rows, :], image_low[rows, :]),
                (text_high[span, :], text_low[span, :]),
                FEATURES,
            )
            score = temperature * score + bias
            if pair % 2 == 0 and chunk >= 2:
                start = own + pair // 2 * HALF - (chunk - 2) * PAIR
                row = lax.broadcasted_iota(jnp.int32, (PAIR, PAIR), 0) - start
                column = lax.broadcasted_iota(jnp.int32, (PAIR, PAIR), 1)
                same = (row == column) & (row >= 0) & (row < HALF)
                slope = 1.0 / (1.0 + jnp.exp(jnp.where(same, score, -score)))
                slope = jnp.where(same, -slope, slope)
            else:
                slope = 1.0 / (1.0 + jnp.exp(-score))
            slope_high[rows, span], slope_low[rows, span] = split(slope)
    copies = []
    for i in range(2):
        rows = pl.ds(i * PAIR, PAIR)
        far[rows, :] = dot3(
            (slope_high[rows, :], slope_low[rows, :]), (text_high[...], text_low[...]), PLAIN
        )
        copy = pltpu.make_async_copy(far.at[rows], far_out.at[rows], sems.at[6 + i])
        copy.start()
        copies.append(copy)
    for copy in copies:
        copy.wait()


def slopes(scalars, place, image, texts):
    texts = [*kept(texts[: LATE[0]]), *texts[LATE[0] :]]
    return pl.pallas_call(
        slopes_kernel,
        out_shape=(pltpu.HBM((NEAR, D), F32),)
        + (vmem(SIDE, D, BF16),) * 4
        + (vmem(SIDE, SIDE, BF16),) * 2,
        in_specs=[SCALARS, SCALARS, ANY_SPACE] + [ANY_SPACE if k in LATE else VECTORS for k in range(8)],
        out_specs=[ANY_SPACE] + [VECTORS] * 6,
        scratch_shapes=[
            vmem(SIDE),
            vmem(3 * BUNDLE),
            vmem(NEAR),
            pltpu.SemaphoreType.DMA((11,)),
        ],
        compiler_params=params(20),
        cost_estimate=pl.CostEstimate(
            flops=9 * SIDE * SIDE * D, bytes_accessed=10 << 20, transcendentals=2 * SIDE * SIDE
        ),
    )(scalars, place, *outside([image]), *texts)


def near_kernel(arrived, text_high, text_low, slope_high, slope_low, out, total, sems):
    copies = []
    for i in range(2):
        rows = pl.ds(i * PAIR, PAIR)
        near = pl.ds(NEAR + i * PAIR, PAIR)
        direction = dot3(
            (slope_high[near, :], slope_low[near, :]), (text_high[...], text_low[...]), PLAIN
        )
        total[rows, :] = arrived[rows, :] + direction
        copy = pltpu.make_async_copy(total.at[rows], out.at[rows], sems.at[i])
        copy.start()
        copies.append(copy)
    for copy in copies:
        copy.wait()


def near_directions(arrived, slope_parts, text_parts):
    return pl.pallas_call(
        near_kernel,
        out_shape=pltpu.HBM((NEAR, D), F32),
        in_specs=[VECTORS] * 5,
        out_specs=ANY_SPACE,
        scratch_shapes=[vmem(NEAR), pltpu.SemaphoreType.DMA((2,))],
        compiler_params=params(12),
        cost_estimate=BRIEF,
    )(*kept([arrived, *text_parts, *slope_parts]))


def text_kernel(slope_high, slope_low, image_high, image_low, *refs):
    outs = refs[:8]
    total, sems = refs[8:]
    copies = []
    for pair in range(4):
        span = pl.ds(pair * PAIR, PAIR)
        total[span, :] = dot3(
            (slope_high[:, span], slope_low[:, span]), (image_high[...], image_low[...]), ROWS_ROWS
        )
        for k in (2 * pair, 2 * pair + 1):
            copy = pltpu.make_async_copy(total.at[pl.ds(k * BUNDLE, BUNDLE)], outs[k], sems.at[k])
            copy.start()
            copies.append(copy)
    for copy in copies:
        copy.wait()


def text_directions(slope_parts, image_parts):
    return pl.pallas_call(
        text_kernel,
        out_shape=(pltpu.HBM((BUNDLE, D), F32),) * 8,
        in_specs=[VECTORS] * 4,
        out_specs=[ANY_SPACE] * 8,
        scratch_shapes=[vmem(SIDE), pltpu.SemaphoreType.DMA((8,))],
        compiler_params=params(14),
        cost_estimate=BRIEF,
    )(*kept([*slope_parts, *image_parts]))


def add_kernel(own, first, second, third, *outs):
    for k in range(4):
        rows = pl.ds(k * HALF, HALF)
        outs[k][...] = (own[rows, :] + first[rows, :]) + (second[rows, :] + third[rows, :])


def add_bundles(parts):
    return pl.pallas_call(
        add_kernel,
        out_shape=(vmem(HALF),) * 4,
        in_specs=[VECTORS] * 4,
        out_specs=[VECTORS] * 4,
        compiler_params=params(4),
    )(*kept(parts))


def last_kernel(scalar_ref, image_ref, text_ref, image_hbm, *refs):
    text_sums = refs[:8]
    image_out, text_out, image_sum, sem = refs[8:]
    copy = pltpu.make_async_copy(image_hbm, image_sum, sem)
    copy.start()
    temperature = scalar_ref[0]

    def back_through(rows, direction):
        inverse = inverse_norm(rows)
        unit = rows * inverse
        along = jnp.sum(unit * direction, axis=1, keepdims=True)
        return inverse * (direction - unit * along)

    for k in range(2):
        a, b, c, d = text_sums[4 * k : 4 * k + 4]
        direction = temperature * ((a[...] + b[...]) + (c[...] + d[...]))
        rows = pl.ds((1 - k) * HALF, HALF)
        text_out[rows, :] = back_through(text_ref[rows, :], direction)
    copy.wait()
    image_out[...] = back_through(image_ref[...], temperature * image_sum[...])


def last(scalars, image, text, image_sum, text_sums):
    return pl.pallas_call(
        last_kernel,
        out_shape=(shape(ROWS), shape(ROWS)),
        in_specs=[SCALARS] + [VECTORS] * 2 + [ANY_SPACE] + [VECTORS] * 8,
        out_specs=[VECTORS] * 2,
        scratch_shapes=[vmem(ROWS), pltpu.SemaphoreType.DMA(())],
        compiler_params=params(4),
    )(scalars, image, text, *outside([image_sum]), *kept(text_sums))


def around(shift, values):
    return [shift(value, by) for value, by in zip(values, (1, -1, 2))]


def send_back(y_values, x_values):
    from_y = [shift_y(y_values[2], 1), shift_y(y_values[1], -1)]
    from_x = [shift_x(x_values[2], 1), shift_x(x_values[1], -1)]
    from_y.append(shift_y(y_values[3], 2))
    from_x.append(shift_x(x_values[3], 2))
    return from_y, from_x


def local(image, text, scale_exponent, bias):
    scalars = jnp.concatenate([jnp.exp(scale_exponent), bias])
    core = lax.axis_index("core")
    place = jnp.stack([(1 - core) * NEAR, lax.axis_index("z") * ROWS]).astype(jnp.int32)

    images = lax.all_gather(image, ("core", "z"), axis=0, tiled=True)

    first_half, second_half = text[:HALF], text[HALF:]
    first_bundle = jnp.concatenate([first_half] + around(shift_x, [first_half] * 3), axis=0)
    second_bundle = jnp.concatenate([second_half] + around(shift_y, [second_half] * 3), axis=0)
    first_bundle, second_bundle = lax.optimization_barrier((first_bundle, second_bundle))
    texts = [first_bundle] + around(shift_y, [first_bundle] * 3)
    texts += [second_bundle] + around(shift_x, [second_bundle] * 3)

    far, *parts = slopes(scalars, place, images, texts)
    text_parts, image_parts, slope_parts = parts[:2], parts[2:4], parts[4:]
    arrived = swap_core(far)
    sums = text_directions(slope_parts, image_parts)
    arrived, sums = lax.optimization_barrier((arrived, sums))
    first_sums, second_sums = sums[:4], sums[4:]
    near = near_directions(arrived, slope_parts, text_parts)
    image_sum = lax.psum_scatter(near, "z", scatter_dimension=0, tiled=True)
    first_sent, second_sent = send_back(first_sums, second_sums)
    first_parts = add_bundles([first_sums[0]] + first_sent)
    second_parts = add_bundles([second_sums[0]] + second_sent)
    second_sent, first_sent = send_back(second_parts, first_parts)
    text_sums = [second_parts[0]] + second_sent + [first_parts[0]] + first_sent
    return last(scalars, image, text, image_sum, text_sums)


def solution(mesh):
    fine = Mesh(mesh.devices.reshape(2, 8, 2, 4, 2), ("xl", "z", "core", "y", "xh"))
    rows = P(("xl", "z", "core", "y", "xh"), None)
    return jax.shard_map(
        local,
        mesh=fine,
        in_specs=(rows, rows, P(), P()),
        out_specs=(rows, rows),
        check_vma=False,
    )
```

```python
import functools

import jax
import jax.numpy as jnp
from jax import lax
from jax.experimental import pallas as pl
from jax.experimental.pallas import tpu as pltpu
from jax.sharding import Mesh, PartitionSpec as P

EPSILON = 1e-06
D = 1152
ROWS = 64
HALF = 32
BUNDLE = 128
SIDE = 1024
NEAR = 512
PAIR = 256
F32 = jnp.float32
BF16 = jnp.bfloat16
ROWS_ROWS = (((0,), (0,)), ((), ()))
FEATURES = (((1,), (1,)), ((), ()))
PLAIN = (((1,), (0,)), ((), ()))
EARLY = (0, 1, 2, 3, 4)
LATE = (5, 6, 7)
COLUMNS = (pl.ds(0, 512), pl.ds(512, 512), pl.ds(1024, 128))
RING_X = ("xl", "xh")


def x_index(place):
    return (place % 2) * 2 + place // 2


def shift_x(value, by):
    return lax.ppermute(value, RING_X, [(x_index(i), x_index((i + by) % 4)) for i in range(4)])


def shift_y(value, by):
    return lax.ppermute(value, "y", [(i, (i + by) % 4) for i in range(4)])


def swap_core(value):
    return lax.ppermute(value, "core", [(0, 1), (1, 0)])


def split(value):
    high = value.astype(BF16)
    low = (value - high.astype(F32)).astype(BF16)
    return high, low


def dot3(left, right, dims):
    dot = functools.partial(lax.dot_general, dimension_numbers=dims, preferred_element_type=F32)
    return dot(left[0], right[0]) + (dot(left[0], right[1]) + dot(left[1], right[0]))


def inverse_norm(rows):
    return lax.rsqrt(jnp.sum(rows * rows, axis=1, keepdims=True) + EPSILON)


def params(mebibytes):
    return pltpu.CompilerParams(vmem_limit_bytes=mebibytes * 1024 * 1024)


def shape(rows, columns=D, dtype=F32):
    return jax.ShapeDtypeStruct((rows, columns), dtype)


def vmem(rows, columns=D, dtype=F32):
    return pltpu.VMEM((rows, columns), dtype)


def kept(values):
    return [pltpu.with_memory_space_constraint(value, pltpu.VMEM) for value in values]


def outside(values):
    return [pltpu.with_memory_space_constraint(value, pltpu.HBM) for value in values]


ANY_SPACE = pl.BlockSpec(memory_space=pl.ANY)
SCALARS = pl.BlockSpec(memory_space=pltpu.SMEM)
VECTORS = pl.BlockSpec(memory_space=pltpu.VMEM)


BRIEF = pl.CostEstimate(flops=SIDE, bytes_accessed=SIDE, transcendentals=0)


def split_units(rows):
    return split(rows * inverse_norm(rows))


def slopes_kernel(scalar_ref, place_ref, image_hbm, *refs):
    texts = refs[:8]
    far_out, text_high, text_low, image_high, image_low, slope_high, slope_low = refs[8:15]
    image, late, far, sems = refs[15:]
    own = place_ref[1]
    late_copies = []
    for k in range(len(LATE)):
        copy = pltpu.make_async_copy(
            texts[LATE[k]], late.at[pl.ds(k * BUNDLE, BUNDLE)], sems.at[8 + k]
        )
        copy.start()
        late_copies.append(copy)
    image_copies = []
    for chunk in range(4):
        first = pl.multiple_of((place_ref[0] + chunk * PAIR) % SIDE, PAIR)
        copy = pltpu.make_async_copy(
            image_hbm.at[pl.ds(first, PAIR)], image.at[pl.ds(chunk * PAIR, PAIR)], sems.at[chunk]
        )
        copy.start()
        image_copies.append(copy)
    temperature = scalar_ref[0]
    bias = scalar_ref[1]
    for bundle in EARLY:
        rows = pl.ds(bundle * BUNDLE, BUNDLE)
        text_high[rows, :], text_low[rows, :] = split_units(texts[bundle][...])
    for copy in late_copies:
        copy.wait()
    for k, bundle in enumerate(LATE):
        rows = pl.ds(bundle * BUNDLE, BUNDLE)
        text_high[rows, :], text_low[rows, :] = split_units(late[pl.ds(k * BUNDLE, BUNDLE), :])
    for chunk in range(4):
        rows = pl.ds(chunk * PAIR, PAIR)
        image_copies[chunk].wait()
        image_high[rows, :], image_low[rows, :] = split_units(image[rows, :])
        for pair in range(4):
            span = pl.ds(pair * PAIR, PAIR)
            score = dot3(
                (image_high[rows, :], image_low[rows, :]),
                (text_high[span, :], text_low[span, :]),
                FEATURES,
            )
            score = temperature * score + bias
            if pair % 2 == 0 and chunk >= 2:
                start = own + pair // 2 * HALF - (chunk - 2) * PAIR
                row = lax.broadcasted_iota(jnp.int32, (PAIR, PAIR), 0) - start
                column = lax.broadcasted_iota(jnp.int32, (PAIR, PAIR), 1)
                same = (row == column) & (row >= 0) & (row < HALF)
                slope = 1.0 / (1.0 + jnp.exp(jnp.where(same, score, -score)))
                slope = jnp.where(same, -slope, slope)
            else:
                slope = 1.0 / (1.0 + jnp.exp(-score))
            slope_high[rows, span], slope_low[rows, span] = split(slope)
    copies = []
    rows = pl.ds(0, NEAR)
    for i, columns in enumerate(COLUMNS):
        far[:, columns] = dot3(
            (slope_high[rows, :], slope_low[rows, :]),
            (text_high[:, columns], text_low[:, columns]),
            PLAIN,
        )
        copy = pltpu.make_async_copy(far.at[:, columns], far_out.at[:, columns], sems.at[11 + i])
        copy.start()
        copies.append(copy)
    for copy in copies:
        copy.wait()


def slopes(scalars, place, image, texts):
    texts = [*kept(texts[: LATE[0]]), *texts[LATE[0] :]]
    return pl.pallas_call(
        slopes_kernel,
        out_shape=(pltpu.HBM((NEAR, D), F32),)
        + (vmem(SIDE, D, BF16),) * 4
        + (vmem(SIDE, SIDE, BF16),) * 2,
        in_specs=[SCALARS, SCALARS, ANY_SPACE] + [ANY_SPACE if k in LATE else VECTORS for k in range(8)],
        out_specs=[ANY_SPACE] + [VECTORS] * 6,
        scratch_shapes=[
            vmem(SIDE),
            vmem(3 * BUNDLE),
            vmem(NEAR),
            pltpu.SemaphoreType.DMA((14,)),
        ],
        compiler_params=params(20),
        cost_estimate=pl.CostEstimate(
            flops=9 * SIDE * SIDE * D, bytes_accessed=10 << 20, transcendentals=2 * SIDE * SIDE
        ),
    )(scalars, place, *outside([image]), *texts)


def near_kernel(arrived, text_high, text_low, slope_high, slope_low, out, total, sems):
    copies = []
    near = pl.ds(NEAR, NEAR)
    for i, columns in enumerate(COLUMNS):
        total[:, columns] = arrived[:, columns] + dot3(
            (slope_high[near, :], slope_low[near, :]),
            (text_high[:, columns], text_low[:, columns]),
            PLAIN,
        )
        copy = pltpu.make_async_copy(total.at[:, columns], out.at[:, columns], sems.at[i])
        copy.start()
        copies.append(copy)
    for copy in copies:
        copy.wait()


def near_directions(arrived, slope_parts, text_parts):
    return pl.pallas_call(
        near_kernel,
        out_shape=pltpu.HBM((NEAR, D), F32),
        in_specs=[VECTORS] * 5,
        out_specs=ANY_SPACE,
        scratch_shapes=[vmem(NEAR), pltpu.SemaphoreType.DMA((3,))],
        compiler_params=params(12),
        cost_estimate=BRIEF,
    )(*kept([arrived, *text_parts, *slope_parts]))


def text_kernel(slope_high, slope_low, image_high, image_low, *refs):
    outs = refs[:8]
    total, sems = refs[8:]
    copies = []
    for pair in range(4):
        span = pl.ds(pair * PAIR, PAIR)
        total[span, :] = dot3(
            (slope_high[:, span], slope_low[:, span]), (image_high[...], image_low[...]), ROWS_ROWS
        )
        for k in (2 * pair, 2 * pair + 1):
            copy = pltpu.make_async_copy(total.at[pl.ds(k * BUNDLE, BUNDLE)], outs[k], sems.at[k])
            copy.start()
            copies.append(copy)
    for copy in copies:
        copy.wait()


def text_directions(slope_parts, image_parts):
    return pl.pallas_call(
        text_kernel,
        out_shape=(pltpu.HBM((BUNDLE, D), F32),) * 8,
        in_specs=[VECTORS] * 4,
        out_specs=[ANY_SPACE] * 8,
        scratch_shapes=[vmem(SIDE), pltpu.SemaphoreType.DMA((8,))],
        compiler_params=params(14),
        cost_estimate=BRIEF,
    )(*kept([*slope_parts, *image_parts]))


def add_kernel(own, first, second, third, *outs):
    for k in range(4):
        rows = pl.ds(k * HALF, HALF)
        outs[k][...] = (own[rows, :] + first[rows, :]) + (second[rows, :] + third[rows, :])


def add_bundles(parts):
    return pl.pallas_call(
        add_kernel,
        out_shape=(vmem(HALF),) * 4,
        in_specs=[VECTORS] * 4,
        out_specs=[VECTORS] * 4,
        compiler_params=params(4),
    )(*kept(parts))


def last_kernel(scalar_ref, image_ref, text_ref, image_hbm, *refs):
    text_sums = refs[:8]
    image_out, text_out, image_sum, sem = refs[8:]
    copy = pltpu.make_async_copy(image_hbm, image_sum, sem)
    copy.start()
    temperature = scalar_ref[0]

    def back_through(rows, direction):
        inverse = inverse_norm(rows)
        unit = rows * inverse
        along = jnp.sum(unit * direction, axis=1, keepdims=True)
        return inverse * (direction - unit * along)

    for k in range(2):
        a, b, c, d = text_sums[4 * k : 4 * k + 4]
        direction = temperature * ((a[...] + b[...]) + (c[...] + d[...]))
        rows = pl.ds((1 - k) * HALF, HALF)
        text_out[rows, :] = back_through(text_ref[rows, :], direction)
    copy.wait()
    image_out[...] = back_through(image_ref[...], temperature * image_sum[...])


def last(scalars, image, text, image_sum, text_sums):
    return pl.pallas_call(
        last_kernel,
        out_shape=(shape(ROWS), shape(ROWS)),
        in_specs=[SCALARS] + [VECTORS] * 2 + [ANY_SPACE] + [VECTORS] * 8,
        out_specs=[VECTORS] * 2,
        scratch_shapes=[vmem(ROWS), pltpu.SemaphoreType.DMA(())],
        compiler_params=params(4),
    )(scalars, image, text, *outside([image_sum]), *kept(text_sums))


def around(shift, values):
    return [shift(value, by) for value, by in zip(values, (1, -1, 2))]


def send_back(y_values, x_values):
    from_y = [shift_y(y_values[2], 1), shift_y(y_values[1], -1)]
    from_x = [shift_x(x_values[2], 1), shift_x(x_values[1], -1)]
    from_y.append(shift_y(y_values[3], 2))
    from_x.append(shift_x(x_values[3], 2))
    return from_y, from_x


def local(image, text, scale_exponent, bias):
    scalars = jnp.concatenate([jnp.exp(scale_exponent), bias])
    core = lax.axis_index("core")
    place = jnp.stack([(1 - core) * NEAR, lax.axis_index("z") * ROWS]).astype(jnp.int32)

    images = lax.all_gather(image, ("core", "z"), axis=0, tiled=True)

    first_half, second_half = text[:HALF], text[HALF:]
    first_bundle = jnp.concatenate([first_half] + around(shift_x, [first_half] * 3), axis=0)
    second_bundle = jnp.concatenate([second_half] + around(shift_y, [second_half] * 3), axis=0)
    first_bundle, second_bundle = lax.optimization_barrier((first_bundle, second_bundle))
    texts = [first_bundle] + around(shift_y, [first_bundle] * 3)
    texts += [second_bundle] + around(shift_x, [second_bundle] * 3)

    far, *parts = slopes(scalars, place, images, texts)
    text_parts, image_parts, slope_parts = parts[:2], parts[2:4], parts[4:]
    arrived = swap_core(far)
    sums = text_directions(slope_parts, image_parts)
    arrived, sums = lax.optimization_barrier((arrived, sums))
    first_sums, second_sums = sums[:4], sums[4:]
    near = near_directions(arrived, slope_parts, text_parts)
    image_sum = lax.psum_scatter(near, "z", scatter_dimension=0, tiled=True)
    first_sent, second_sent = send_back(first_sums, second_sums)
    first_parts = add_bundles([first_sums[0]] + first_sent)
    second_parts = add_bundles([second_sums[0]] + second_sent)
    second_sent, first_sent = send_back(second_parts, first_parts)
    text_sums = [second_parts[0]] + second_sent + [first_parts[0]] + first_sent
    return last(scalars, image, text, image_sum, text_sums)


def solution(mesh):
    fine = Mesh(mesh.devices.reshape(2, 8, 2, 4, 2), ("xl", "z", "core", "y", "xh"))
    rows = P(("xl", "z", "core", "y", "xh"), None)
    return jax.shard_map(
        local,
        mesh=fine,
        in_specs=(rows, rows, P(), P()),
        out_specs=(rows, rows),
        check_vma=False,
    )
```
